32 devices in a mesh: draws: 2 (over x), rows: 16 (over z, y, core).
Axes of the slice: x: 2, y: 2, z: 4, core: 2. Of those that a mesh axis runs over, the one named last changes fastest.
Arguments:
- leaf_rhs: bfloat16 [192, 256, 256], P('rows'), may hold values from -6 to 6
- separator_rhs: bfloat16 [4, 16, 256, 256], P(None, 'rows'), may hold values from -6 to 6
- leaf_inverse: bfloat16 [384, 256, 256], P(('draws', 'rows')), parts along dimension 0, as said below
- leaf_factor: bfloat16 [256, 4, 256, 256], P(('draws', 'rows')), parts along dimension 0, may hold values from -0.125 to 0.125
- separator_inverse: bfloat16 [4, 32, 256, 256], P(None, ('draws', 'rows')), parts along dimension 1, as said below
- separator_factor: bfloat16 [4, 32, 2, 256, 256], P(None, ('draws', 'rows')), parts along dimension 1, may hold values from -0.1875 to 0.1875
- block_pattern: int32 [128, 4], P('rows'), may hold values from 0 to 7, as said below
- link_row: int32 [16], P('rows'), may hold values from 8 to 11
Outputs:
- leaf_solution: bfloat16 [384, 256, 256], P(('draws', 'rows')), parts along dimension 0
- separator_solution: bfloat16 [4, 32, 256, 256], P(None, ('draws', 'rows')), parts along dimension 1
The draws below stay inside these ranges and needn't reach their ends.
There are 2 independent parts, one for each index of `draws`. The reference program is written for one: setup_inputs(seed, part) draws one part's arguments, and reference() takes and returns one part's arrays. A program takes and returns all parts, laid end to end along the dimension named above; an argument that names none is the same for every part. Nothing has to cross between parts.
Inputs may be any that keep to these rules, and one draw needn't show every extreme that they name: `block_pattern`: for a block row on leaf level v >= 1 the 4 entries are distinct and below v * 4. `leaf_inverse`: every block is invertible. `separator_inverse`: every block is invertible.
All inputs are finite; a program needn't handle non-finite values.
Results may differ from the reference program's by a relative error of at most 0.011.
Values may be sent and summed in bfloat16 or wider, within the bound.
A program may use at most 64 MiB of HBM per device.

```python
import math
import jax
import jax.numpy as jnp
from jax import lax

BLOCK = 256
LOADS = 256
LEVEL_ROWS = 4
LEAF_LEVELS = 3
COUPLED = 4
LOCAL = 12
UPPER = 8
LEAF_ROWS = 192
TREE_DEPTH = 4
N_ROWS = 16


def draw_dominant(key, count):
    key_diag, key_off = jax.random.split(key)
    diagonal_part = jnp.exp(jax.random.uniform(key_diag, (count, BLOCK), jnp.float32, math.log(0.5), math.log(1.5)))
    off_part = jax.random.normal(key_off, (count, BLOCK, BLOCK), jnp.float32) * (0.4 / math.sqrt(BLOCK))
    identity = jnp.eye(BLOCK, dtype=jnp.float32)
    return (off_part + identity[None, :, :] * diagonal_part[:, :, None]).astype(jnp.bfloat16)


def draw_leaf_inverse(key, part):
    return draw_dominant(jax.random.fold_in(key, 11), N_ROWS * LOCAL)


def draw_separator_inverse(key, part):
    return draw_dominant(jax.random.fold_in(key, 23), TREE_DEPTH * N_ROWS).reshape(TREE_DEPTH, N_ROWS, BLOCK, BLOCK)


def draw_block_pattern(key, part):
    total_rows = N_ROWS * UPPER
    scores = jax.random.randint(jax.random.fold_in(key, 37), (total_rows, UPPER), 0, 2 ** 20, dtype=jnp.int32)
    column = jnp.arange(UPPER, dtype=jnp.int32)[None, :]
    leaf_level = jnp.arange(total_rows, dtype=jnp.int32) % UPPER // LEVEL_ROWS + 1
    available = (leaf_level * LEVEL_ROWS)[:, None]
    keyed = scores * UPPER + column + jnp.where(column >= available, 2 ** 30, 0).astype(jnp.int32)
    ordered = jnp.argsort(keyed, axis=1, stable=True)
    return ordered[:, :COUPLED].astype(jnp.int32)


def place_ends(values, own_key, low, top_value):
    spot = [jax.random.randint(jax.random.fold_in(own_key, axis), (), 0, length) for axis, length in enumerate(values.shape)]
    longest = values.shape.index(max(values.shape))
    neighbour = spot[:longest] + [(spot[longest] + 1) % values.shape[longest]] + spot[longest + 1:]
    return values.at[tuple(spot)].set(low).at[tuple(neighbour)].set(top_value)


def block_scale(own_key, extent, shards, smallest, largest):
    def one(position, shards_of):
        steps = jax.random.uniform(jax.random.fold_in(jax.random.fold_in(own_key, 6), position), (shards_of,), jnp.float32, smallest / len(shards), largest / len(shards))
        return jnp.repeat(jnp.exp(steps), extent[position] // shards_of).reshape((-1,) + (1,) * (len(extent) - position - 1))

    level = one(*shards[0])
    for cut in shards[1:]:
        level = level * one(*cut)
    return level


def scatter_about(own_key, shape, spread, bound, cuts=(), held_as=jnp.bfloat16):
    level = block_scale(own_key, shape, cuts, -0.22, 0.18) if cuts else 1.0
    result = jax.random.normal(own_key, shape, jnp.float32) * spread * level
    return jnp.minimum(jnp.maximum(result, -bound), bound).astype(held_as)


def setup_inputs(seed: int = 0, part: int = 0) -> dict:
    key_of = jax.random.split(jax.random.key(seed), 9)
    own_keys = jax.random.split(jax.random.fold_in(key_of[8], part), 9)
    return {
        "leaf_rhs": scatter_about(key_of[0], (LEAF_ROWS, BLOCK, LOADS), 1.0, 6.0, ((0, 16),)),
        "separator_rhs": scatter_about(key_of[1], (TREE_DEPTH, N_ROWS, BLOCK, LOADS), 1.0, 6.0, ((1, 16),)),
        "leaf_inverse": draw_leaf_inverse(jax.random.fold_in(jax.random.fold_in(key_of[8], part), 71), part),
        "leaf_factor": scatter_about(own_keys[3], (UPPER * N_ROWS, COUPLED, BLOCK, BLOCK), (2 * COUPLED * BLOCK) ** -0.5, 0.125, ((0, 16),)),
        "separator_inverse": draw_separator_inverse(jax.random.fold_in(jax.random.fold_in(key_of[8], part), 71), part),
        "separator_factor": scatter_about(own_keys[5], (TREE_DEPTH, N_ROWS, 2, BLOCK, BLOCK), (4 * BLOCK) ** -0.5, 0.1875, ((1, 16),)),
        "block_pattern": draw_block_pattern(jax.random.fold_in(key_of[8], 71), part),
        "link_row": place_ends(jax.random.randint(key_of[7], (N_ROWS,), UPPER, LOCAL), jax.random.fold_in(key_of[7], 1), UPPER, LOCAL - 1).astype(jnp.int32),
    }


def solve_leaf(leaf_items):
    rhs_one, inverse_one, factor_one, pattern_one = leaf_items
    solved = jnp.einsum("nij,njr->nir", inverse_one[:LEVEL_ROWS].astype(jnp.float32), rhs_one[:LEVEL_ROWS].astype(jnp.float32)).astype(jnp.bfloat16)
    for height in range(1, LEAF_LEVELS):
        low_row = (height - 1) * LEVEL_ROWS
        top_row = height * LEVEL_ROWS
        picked = jnp.take(solved, pattern_one[low_row:top_row], axis=0)
        accumulated = jnp.einsum("nkij,nkjr->nir", factor_one[low_row:top_row].astype(jnp.float32), picked.astype(jnp.float32))
        residual = (rhs_one[top_row:top_row + LEVEL_ROWS].astype(jnp.float32) - accumulated).astype(jnp.bfloat16)
        fresh_rows = jnp.einsum("nij,njr->nir", inverse_one[top_row:top_row + LEVEL_ROWS].astype(jnp.float32), residual.astype(jnp.float32)).astype(jnp.bfloat16)
        solved = jnp.concatenate([solved, fresh_rows], axis=0)
    return solved


def solve_level(lower_in, upper_in, rhs_level, inverse_level, factor_level):
    factors = factor_level.astype(jnp.float32)
    accumulated = jnp.einsum("nij,njr->nir", factors[:, 0], lower_in.astype(jnp.float32)) + jnp.einsum("nij,njr->nir", factors[:, 1], upper_in.astype(jnp.float32))
    residual = (rhs_level.astype(jnp.float32) - accumulated).astype(jnp.bfloat16)
    return jnp.einsum("nij,njr->nir", inverse_level.astype(jnp.float32), residual.astype(jnp.float32)).astype(jnp.bfloat16)


def reference(leaf_rhs, separator_rhs, leaf_inverse, leaf_factor, separator_inverse, separator_factor, block_pattern, link_row):
    leaf_items = (leaf_rhs.reshape(N_ROWS, LOCAL, BLOCK, LOADS), leaf_inverse.reshape(N_ROWS, LOCAL, BLOCK, BLOCK), leaf_factor.reshape(N_ROWS, UPPER, COUPLED, BLOCK, BLOCK), block_pattern.reshape(N_ROWS, UPPER, COUPLED))
    solved = lax.map(solve_leaf, leaf_items)
    edges = solved[jnp.arange(N_ROWS, dtype=jnp.int32), link_row]
    level_block = solve_level(jnp.roll(edges, 1, axis=0), edges, separator_rhs[0], separator_inverse[0], separator_factor[0])
    levels = [level_block]
    for height in range(1, TREE_DEPTH):
        stride = 2 ** (height - 1)
        level_block = solve_level(jnp.roll(level_block, stride, axis=0), jnp.roll(level_block, -stride, axis=0), separator_rhs[height], separator_inverse[height], separator_factor[height])
        levels.append(level_block)
    return solved.reshape(N_ROWS * LOCAL, BLOCK, LOADS), jnp.stack(levels, axis=0)
```

```python
import functools

import jax
import jax.numpy as jnp
from jax import lax
from jax.experimental import pallas as pl
from jax.experimental.pallas import tpu as pltpu
from jax.sharding import PartitionSpec as P

LEVEL_ROWS = 4
LEAF_LEVELS = 3
CHUNKS = 2
F32 = jnp.float32
BF16 = jnp.bfloat16


def dot(a, b):
    return jnp.dot(a, b, preferred_element_type=F32)


def kernel(
    n,
    depth,
    relay_level,
    rhs_hbm,
    sep_rhs_hbm,
    inv_hbm,
    fac_hbm,
    sep_inv_hbm,
    sep_fac_hbm,
    pattern,
    link,
    leaf_out,
    sep_out,
    rhs,
    inv,
    fac,
    sep_rhs,
    sep_inv,
    sep_fac,
    solved,
    edge,
    sol,
    recv,
    load_sem,
    leaf_sem,
    out_sem,
    send_sem,
    recv_sem,
):
    me = lax.axis_index("rows")
    coupled = fac.shape[1]
    width = sol.shape[-1]

    def peer(by):
        return lax.rem(me + (by % n), n)

    loads = {}

    def load(name, src, dst):
        copy = pltpu.make_async_copy(src, dst, load_sem.at[len(loads)])
        copy.start()
        loads[name] = copy

    for level in range(LEAF_LEVELS):
        rows = pl.ds(level * LEVEL_ROWS, LEVEL_ROWS)
        if level:
            low = pl.ds((level - 1) * LEVEL_ROWS, LEVEL_ROWS)
            load(("fac", level), fac_hbm.at[low], fac.at[low])
        load(("rhs", level), rhs_hbm.at[rows], rhs.at[rows])
        load(("inv", level), inv_hbm.at[rows], inv.at[rows])
    load("sep_fac", sep_fac_hbm.at[:, 0], sep_fac)
    load("sep_rhs", sep_rhs_hbm.at[:, 0], sep_rhs)
    load("sep_inv", sep_inv_hbm.at[:, 0], sep_inv)

    offsets = sorted({(sign * 2**h) % n for h in range(depth - 1) for sign in (1, -1)})
    barrier = pltpu.get_barrier_semaphore()
    for by in offsets:
        pl.semaphore_signal(
            barrier, inc=1, device_id={"rows": peer(by)}, device_id_type=pl.DeviceIdType.MESH
        )

    def residual(row, q):
        total = dot(fac[q, 0], solved[pattern[q, 0]])
        for k in range(1, coupled):
            total += dot(fac[q, k], solved[pattern[q, k]])
        return (rhs[row].astype(F32) - total).astype(BF16)

    out_copies = []

    def leaf_write(level):
        rows = pl.ds(level * LEVEL_ROWS, LEVEL_ROWS)
        copy = pltpu.make_async_copy(solved.at[rows], leaf_out.at[rows], leaf_sem.at[level])
        copy.start()
        out_copies.append(copy)

    loads[("rhs", 0)].wait()
    loads[("inv", 0)].wait()
    for row in range(LEVEL_ROWS):
        solved[row] = dot(inv[row], rhs[row]).astype(BF16)
    leaf_write(0)

    def leaf_level(level):
        first = level * LEVEL_ROWS
        parts = [residual(first + i, first - LEVEL_ROWS + i) for i in range(LEVEL_ROWS)]
        for i in range(LEVEL_ROWS):
            solved[first + i] = dot(inv[first + i], parts[i]).astype(BF16)
        leaf_write(level)

    for level in range(1, LEAF_LEVELS - 1):
        for name in ("fac", "rhs", "inv"):
            loads[(name, level)].wait()
        leaf_level(level)

    top = LEAF_LEVELS - 1
    for name in ("fac", "rhs", "inv"):
        loads[(name, top)].wait()
    link_row = link[0]
    edge_block = dot(inv[link_row], residual(link_row, jnp.maximum(link_row - LEVEL_ROWS, 0))).astype(BF16)
    for j in range(CHUNKS):
        edge[j] = edge_block[:, j * width : (j + 1) * width]

    pl.semaphore_wait(barrier, len(offsets))

    sends = []

    def send(src, level, side, j, to, slot):
        copy = pltpu.make_async_remote_copy(
            src_ref=src,
            dst_ref=recv.at[level, side, j],
            send_sem=send_sem.at[level, slot, j],
            recv_sem=recv_sem.at[level, side, j],
            device_id={"rows": to},
            device_id_type=pl.DeviceIdType.MESH,
        )
        copy.start()
        sends.append(copy)

    def arrived(level, side, j):
        pltpu.make_async_remote_copy(
            src_ref=edge.at[j],
            dst_ref=recv.at[level, side, j],
            send_sem=send_sem.at[level, 0, j],
            recv_sem=recv_sem.at[level, side, j],
            device_id={"rows": peer(1)},
            device_id_type=pl.DeviceIdType.MESH,
        ).wait_recv()

    for j in range(CHUNKS):
        send(edge.at[j], 0, 0, j, peer(1), 0)

    leaf_level(top)

    loads["sep_fac"].wait()
    loads["sep_rhs"].wait()
    loads["sep_inv"].wait()

    y = lax.rem(lax.div(me, 2), 2)
    for level in range(depth):
        for j in range(CHUNKS):
            columns = slice(j * width, (j + 1) * width)
            if level == 0:
                total = dot(sep_fac[level, 1], edge[j])
                arrived(level, 0, j)
                total += dot(sep_fac[level, 0], recv[level, 0, j])
            elif level == relay_level:
                stride = 2 ** (level - 1)
                near, far = 1 - y, y
                arrived(level, near, j)
                beyond = lax.rem(me + 2 * stride + (n - 4 * stride) * y, n)
                send(recv.at[level, near, j], level, far, j, beyond, 1)
                total = dot(sep_fac[level, near], recv[level, near, j])
                arrived(level, far, j)
                total += dot(sep_fac[level, far], recv[level, far, j])
            else:
                arrived(level, 0, j)
                total = dot(sep_fac[level, 0], recv[level, 0, j])
                arrived(level, 1, j)
                total += dot(sep_fac[level, 1], recv[level, 1, j])
            part = (sep_rhs[level, :, columns].astype(F32) - total).astype(BF16)
            sol[level, j] = dot(sep_inv[level], part).astype(BF16)
            if level + 1 < depth:
                stride = 2**level
                if level + 1 == relay_level:
                    across = lax.rem(me + stride + (n - 2 * stride) * y, n)
                    send(sol.at[level, j], level + 1, y, j, across, 0)
                else:
                    send(sol.at[level, j], level + 1, 0, j, peer(stride), 0)
                    send(sol.at[level, j], level + 1, 1, j, peer(-stride), 1)
            copy = pltpu.make_async_copy(
                sol.at[level, j], sep_out.at[level, 0, :, pl.ds(j * width, width)], out_sem.at[level, j]
            )
            copy.start()
            out_copies.append(copy)

    for copy in sends:
        copy.wait_send()
    for copy in out_copies:
        copy.wait()


def shards(n, leaf_rhs, separator_rhs, leaf_inverse, leaf_factor, separator_inverse, separator_factor, block_pattern, link_row):
    depth = separator_rhs.shape[0]
    block, loads = leaf_rhs.shape[1:]
    width = loads // CHUNKS
    upper, coupled = leaf_factor.shape[:2]
    matmuls = leaf_rhs.shape[0] + upper * coupled + 3 * depth
    hbm = pl.BlockSpec(memory_space=pl.ANY)
    smem = pl.BlockSpec(memory_space=pltpu.SMEM)
    return pl.pallas_call(
        functools.partial(kernel, n, depth, 2 if n == 16 else -1),
        out_shape=(
            jax.ShapeDtypeStruct(leaf_rhs.shape, BF16),
            jax.ShapeDtypeStruct(separator_rhs.shape, BF16),
        ),
        in_specs=[hbm] * 6 + [smem] * 2,
        out_specs=(hbm, hbm),
        scratch_shapes=[
            pltpu.VMEM(leaf_rhs.shape, BF16),
            pltpu.VMEM(leaf_inverse.shape, BF16),
            pltpu.VMEM(leaf_factor.shape, BF16),
            pltpu.VMEM((depth, block, loads), BF16),
            pltpu.VMEM((depth, block, block), BF16),
            pltpu.VMEM((depth, 2, block, block), BF16),
            pltpu.VMEM(leaf_rhs.shape, BF16),
            pltpu.VMEM((CHUNKS, block, width), BF16),
            pltpu.VMEM((depth, CHUNKS, block, width), BF16),
            pltpu.VMEM((depth, 2, CHUNKS, block, width), BF16),
            pltpu.SemaphoreType.DMA((3 * LEAF_LEVELS + 2,)),
            pltpu.SemaphoreType.DMA((LEAF_LEVELS,)),
            pltpu.SemaphoreType.DMA((depth, CHUNKS)),
            pltpu.SemaphoreType.DMA((depth, 2, CHUNKS)),
            pltpu.SemaphoreType.DMA((depth, 2, CHUNKS)),
        ],
        compiler_params=pltpu.CompilerParams(
            collective_id=0, has_side_effects=True, vmem_limit_bytes=48 * 2**20
        ),
        cost_estimate=pl.CostEstimate(
            flops=2 * matmuls * block * block * loads,
            bytes_accessed=2 * (matmuls + 2 * leaf_rhs.shape[0]) * block * loads,
            transcendentals=0,
        ),
        name="tree_solve",
    )(leaf_rhs, separator_rhs, leaf_inverse, leaf_factor, separator_inverse, separator_factor, block_pattern, link_row)


def solution(mesh):
    placed = (
        P("rows", None, None),
        P(None, "rows", None, None),
        P(("draws", "rows"), None, None),
        P(("draws", "rows"), None, None, None),
        P(None, ("draws", "rows"), None, None),
        P(None, ("draws", "rows"), None, None, None),
        P("rows", None),
        P("rows"),
    )
    return jax.shard_map(
        functools.partial(shards, mesh.shape["rows"]),
        mesh=mesh,
        in_specs=placed,
        out_specs=(P(("draws", "rows"), None, None), P(None, ("draws", "rows"), None, None)),
        check_vma=False,
    )
```

```python
import functools

import jax
import jax.numpy as jnp
from jax import lax
from jax.experimental import pallas as pl
from jax.experimental.pallas import tpu as pltpu
from jax.sharding import PartitionSpec as P

LEVEL_ROWS = 4
LEAF_LEVELS = 3
CHUNKS = 2
F32 = jnp.float32
BF16 = jnp.bfloat16


def dot(a, b):
    return jnp.dot(a, b, preferred_element_type=F32)


def kernel(
    n,
    depth,
    relay_level,
    rhs_hbm,
    sep_rhs_hbm,
    inv_hbm,
    fac_hbm,
    sep_inv_hbm,
    sep_fac_hbm,
    pattern,
    link,
    leaf_out,
    sep_out,
    rhs,
    inv,
    fac,
    sep_rhs,
    sep_inv,
    sep_fac,
    solved,
    edge,
    weight,
    free,
    sol,
    recv,
    load_sem,
    leaf_sem,
    out_sem,
    send_sem,
    recv_sem,
):
    me = lax.axis_index("rows")
    coupled = fac.shape[1]
    width = sol.shape[-1]

    def peer(by):
        return lax.rem(me + (by % n), n)

    loads = {}

    def load(name, src, dst):
        copy = pltpu.make_async_copy(src, dst, load_sem.at[len(loads)])
        copy.start()
        loads[name] = copy

    for level in range(LEAF_LEVELS):
        rows = pl.ds(level * LEVEL_ROWS, LEVEL_ROWS)
        if level:
            low = pl.ds((level - 1) * LEVEL_ROWS, LEVEL_ROWS)
            load(("fac", level), fac_hbm.at[low], fac.at[low])
        load(("rhs", level), rhs_hbm.at[rows], rhs.at[rows])
        load(("inv", level), inv_hbm.at[rows], inv.at[rows])
    load("sep_fac", sep_fac_hbm.at[:, 0], sep_fac)
    load("sep_rhs", sep_rhs_hbm.at[:, 0], sep_rhs)
    load("sep_inv", sep_inv_hbm.at[:, 0], sep_inv)

    offsets = sorted({(sign * 2**h) % n for h in range(depth - 1) for sign in (1, -1)})
    barrier = pltpu.get_barrier_semaphore()
    for by in offsets:
        pl.semaphore_signal(
            barrier, inc=1, device_id={"rows": peer(by)}, device_id_type=pl.DeviceIdType.MESH
        )

    def residual(row, q):
        total = dot(fac[q, 0], solved[pattern[0, q]])
        for k in range(1, coupled):
            total += dot(fac[q, k], solved[pattern[k, q]])
        return (rhs[row].astype(F32) - total).astype(BF16)

    out_copies = []

    def leaf_write(level):
        rows = pl.ds(level * LEVEL_ROWS, LEVEL_ROWS)
        copy = pltpu.make_async_copy(solved.at[rows], leaf_out.at[rows], leaf_sem.at[level])
        copy.start()
        out_copies.append(copy)

    loads[("rhs", 0)].wait()
    loads[("inv", 0)].wait()
    for row in range(LEVEL_ROWS):
        solved[row] = dot(inv[row], rhs[row]).astype(BF16)
    leaf_write(0)

    def leaf_level(level):
        first = level * LEVEL_ROWS
        parts = [residual(first + i, first - LEVEL_ROWS + i) for i in range(LEVEL_ROWS)]
        for i in range(LEVEL_ROWS):
            solved[first + i] = dot(inv[first + i], parts[i]).astype(BF16)
        leaf_write(level)

    for level in range(1, LEAF_LEVELS - 1):
        for name in ("fac", "rhs", "inv"):
            loads[(name, level)].wait()
        leaf_level(level)

    top = LEAF_LEVELS - 1
    for name in ("fac", "rhs", "inv"):
        loads[(name, top)].wait()
    link_row = link[0]
    edge_block = dot(inv[link_row], residual(link_row, jnp.maximum(link_row - LEVEL_ROWS, 0))).astype(BF16)
    for j in range(CHUNKS):
        edge[j] = edge_block[:, j * width : (j + 1) * width]

    pl.semaphore_wait(barrier, len(offsets))

    sends = []

    def send(src, level, side, j, to, slot):
        copy = pltpu.make_async_remote_copy(
            src_ref=src,
            dst_ref=recv.at[level, side, j],
            send_sem=send_sem.at[level, slot, j],
            recv_sem=recv_sem.at[level, side, j],
            device_id={"rows": to},
            device_id_type=pl.DeviceIdType.MESH,
        )
        copy.start()
        sends.append(copy)

    def arrived(level, side, j):
        pltpu.make_async_remote_copy(
            src_ref=edge.at[j],
            dst_ref=recv.at[level, side, j],
            send_sem=send_sem.at[level, 0, j],
            recv_sem=recv_sem.at[level, side, j],
            device_id={"rows": peer(1)},
            device_id_type=pl.DeviceIdType.MESH,
        ).wait_recv()

    for j in range(CHUNKS):
        send(edge.at[j], 0, 0, j, peer(1), 0)

    def prepare(level):
        node_inv = sep_inv[level]
        for side in range(2):
            weight[level, side] = dot(node_inv, sep_fac[level, side]).astype(BF16)
        free[level] = dot(node_inv, sep_rhs[level])

    loads["sep_fac"].wait()
    loads["sep_rhs"].wait()
    loads["sep_inv"].wait()
    prepare(0)

    for level in range(depth):
        stride = 2 ** max(level - 1, 0)
        p = lax.rem(lax.div(me, stride), 2)
        near, far = 1 - p, p
        for j in range(CHUNKS):
            columns = slice(j * width, (j + 1) * width)
            if level == 0:
                total = dot(weight[level, 1], edge[j])
                arrived(level, 0, j)
                total += dot(weight[level, 0], recv[level, 0, j])
            else:
                arrived(level, near, j)
                if level == relay_level:
                    beyond = lax.rem(me + 2 * stride + (n - 4 * stride) * p, n)
                    send(recv.at[level, near, j], level, far, j, beyond, 1)
                total = dot(weight[level, near], recv[level, near, j])
                arrived(level, far, j)
                total += dot(weight[level, far], recv[level, far, j])
            sol[level, j] = (free[level, :, columns] - total).astype(BF16)
            if level + 1 < depth:
                step = 2**level
                q = lax.rem(lax.div(me, step), 2)
                up, down = peer(step), peer(-step)
                if level + 1 == relay_level:
                    send(sol.at[level, j], level + 1, q, j, up + (down - up) * q, 0)
                else:
                    send(sol.at[level, j], level + 1, 1 - q, j, down + (up - down) * q, 0)
                    send(sol.at[level, j], level + 1, q, j, up + (down - up) * q, 1)
            copy = pltpu.make_async_copy(
                sol.at[level, j], sep_out.at[level, 0, :, pl.ds(j * width, width)], out_sem.at[level, j]
            )
            copy.start()
            out_copies.append(copy)
        if level + 1 < depth:
            prepare(level + 1)
        if level == 0:
            leaf_level(top)

    for copy in sends:
        copy.wait_send()
    for copy in out_copies:
        copy.wait()


def shards(n, leaf_rhs, separator_rhs, leaf_inverse, leaf_factor, separator_inverse, separator_factor, block_pattern, link_row):
    depth = separator_rhs.shape[0]
    block, loads = leaf_rhs.shape[1:]
    width = loads // CHUNKS
    upper, coupled = leaf_factor.shape[:2]
    matmuls = leaf_rhs.shape[0] + upper * coupled + 5 * depth
    hbm = pl.BlockSpec(memory_space=pltpu.HBM)
    smem = pl.BlockSpec(memory_space=pltpu.SMEM)
    return pl.pallas_call(
        functools.partial(kernel, n, depth, 2 if n == 16 else -1),
        out_shape=(
            jax.ShapeDtypeStruct(leaf_rhs.shape, BF16),
            jax.ShapeDtypeStruct(separator_rhs.shape, BF16),
        ),
        in_specs=[hbm] * 6 + [smem] * 2,
        out_specs=(hbm, hbm),
        scratch_shapes=[
            pltpu.VMEM(leaf_rhs.shape, BF16),
            pltpu.VMEM(leaf_inverse.shape, BF16),
            pltpu.VMEM(leaf_factor.shape, BF16),
            pltpu.VMEM((depth, block, loads), BF16),
            pltpu.VMEM((depth, block, block), BF16),
            pltpu.VMEM((depth, 2, block, block), BF16),
            pltpu.VMEM(leaf_rhs.shape, BF16),
            pltpu.VMEM((CHUNKS, block, width), BF16),
            pltpu.VMEM((depth, 2, block, block), BF16),
            pltpu.VMEM((depth, block, loads), F32),
            pltpu.VMEM((depth, CHUNKS, block, width), BF16),
            pltpu.VMEM((depth, 2, CHUNKS, block, width), BF16),
            pltpu.SemaphoreType.DMA((3 * LEAF_LEVELS + 2,)),
            pltpu.SemaphoreType.DMA((LEAF_LEVELS,)),
            pltpu.SemaphoreType.DMA((depth, CHUNKS)),
            pltpu.SemaphoreType.DMA((depth, 2, CHUNKS)),
            pltpu.SemaphoreType.DMA((depth, 2, CHUNKS)),
        ],
        compiler_params=pltpu.CompilerParams(
            collective_id=0, has_side_effects=True, vmem_limit_bytes=64 * 2**20
        ),
        cost_estimate=pl.CostEstimate(
            flops=2 * matmuls * block * block * loads,
            bytes_accessed=2 * (matmuls + 2 * leaf_rhs.shape[0]) * block * loads,
            transcendentals=0,
        ),
        name="tree_solve",
    )(leaf_rhs, separator_rhs, leaf_inverse, leaf_factor, separator_inverse, separator_factor, block_pattern.T, link_row)


def solution(mesh):
    placed = (
        P("rows", None, None),
        P(None, "rows", None, None),
        P(("draws", "rows"), None, None),
        P(("draws", "rows"), None, None, None),
        P(None, ("draws", "rows"), None, None),
        P(None, ("draws", "rows"), None, None, None),
        P("rows", None),
        P("rows"),
    )
    return jax.shard_map(
        functools.partial(shards, mesh.shape["rows"]),
        mesh=mesh,
        in_specs=placed,
        out_specs=(P(("draws", "rows"), None, None), P(None, ("draws", "rows"), None, None)),
        check_vma=False,
    )
```

```python
import functools

import jax
import jax.numpy as jnp
from jax import lax
from jax.experimental import pallas as pl
from jax.experimental.pallas import tpu as pltpu
from jax.sharding import PartitionSpec as P

LEVEL_ROWS = 4
LEAF_LEVELS = 3
CHUNKS = 2
F32 = jnp.float32
BF16 = jnp.bfloat16


def dot(a, b):
    return jnp.dot(a, b, preferred_element_type=F32)


def kernel(
    n,
    depth,
    relay_level,
    rhs_hbm,
    sep_rhs_hbm,
    inv_hbm,
    fac_hbm,
    sep_inv_hbm,
    sep_fac_hbm,
    pattern,
    link,
    leaf_out,
    sep_out,
    rhs,
    inv,
    fac,
    sep_rhs,
    sep_inv,
    sep_fac,
    solved,
    edge,
    weight,
    free,
    sol,
    recv,
    load_sem,
    leaf_sem,
    out_sem,
    send_sem,
    recv_sem,
):
    me = lax.axis_index("rows")
    coupled = fac.shape[1]
    width = sol.shape[-1]

    def peer(by):
        return lax.rem(me + (by % n), n)

    loads = {}

    def load(name, src, dst):
        copy = pltpu.make_async_copy(src, dst, load_sem.at[len(loads)])
        copy.start()
        loads[name] = copy

    for level in range(LEAF_LEVELS):
        rows = pl.ds(level * LEVEL_ROWS, LEVEL_ROWS)
        if level:
            low = pl.ds((level - 1) * LEVEL_ROWS, LEVEL_ROWS)
            load(("fac", level), fac_hbm.at[low], fac.at[low])
        load(("rhs", level), rhs_hbm.at[rows], rhs.at[rows])
        load(("inv", level), inv_hbm.at[rows], inv.at[rows])
    load("sep_fac", sep_fac_hbm.at[:, 0], sep_fac)
    load("sep_rhs", sep_rhs_hbm.at[:, 0], sep_rhs)
    load("sep_inv", sep_inv_hbm.at[:, 0], sep_inv)

    offsets = sorted({(sign * 2**h) % n for h in range(depth - 1) for sign in (1, -1)})
    barrier = pltpu.get_barrier_semaphore()
    for by in offsets:
        pl.semaphore_signal(
            barrier, inc=1, device_id={"rows": peer(by)}, device_id_type=pl.DeviceIdType.MESH
        )

    def residual(row, q):
        total = dot(fac[q, 0], solved[pattern[0, q]])
        for k in range(1, coupled):
            total += dot(fac[q, k], solved[pattern[k, q]])
        return (rhs[row].astype(F32) - total).astype(BF16)

    out_copies = []

    def leaf_write(level):
        rows = pl.ds(level * LEVEL_ROWS, LEVEL_ROWS)
        copy = pltpu.make_async_copy(solved.at[rows], leaf_out.at[rows], leaf_sem.at[level])
        copy.start()
        out_copies.append(copy)

    loads[("rhs", 0)].wait()
    loads[("inv", 0)].wait()
    for row in range(LEVEL_ROWS):
        solved[row] = dot(inv[row], rhs[row]).astype(BF16)
    leaf_write(0)

    def leaf_level(level):
        first = level * LEVEL_ROWS
        parts = [residual(first + i, first - LEVEL_ROWS + i) for i in range(LEVEL_ROWS)]
        for i in range(LEVEL_ROWS):
            solved[first + i] = dot(inv[first + i], parts[i]).astype(BF16)
        leaf_write(level)

    for level in range(1, LEAF_LEVELS - 1):
        for name in ("fac", "rhs", "inv"):
            loads[(name, level)].wait()
        leaf_level(level)

    top = LEAF_LEVELS - 1
    for name in ("fac", "rhs", "inv"):
        loads[(name, top)].wait()
    link_row = link[0]
    edge_block = dot(inv[link_row], residual(link_row, jnp.maximum(link_row - LEVEL_ROWS, 0))).astype(BF16)
    for j in range(CHUNKS):
        edge[j] = edge_block[:, j * width : (j + 1) * width]

    pl.semaphore_wait(barrier, len(offsets))

    sends = []

    def send(src, level, side, j, to, slot):
        copy = pltpu.make_async_remote_copy(
            src_ref=src,
            dst_ref=recv.at[level, side, j],
            send_sem=send_sem.at[level, slot, j],
            recv_sem=recv_sem.at[level, side, j],
            device_id={"rows": to},
            device_id_type=pl.DeviceIdType.MESH,
        )
        copy.start()
        sends.append(copy)

    def arrived(level, side, j):
        pltpu.make_async_remote_copy(
            src_ref=edge.at[j],
            dst_ref=recv.at[level, side, j],
            send_sem=send_sem.at[level, 0, j],
            recv_sem=recv_sem.at[level, side, j],
            device_id={"rows": peer(1)},
            device_id_type=pl.DeviceIdType.MESH,
        ).wait_recv()

    for j in range(CHUNKS):
        send(edge.at[j], 0, 0, j, peer(1), 0)

    def prepare(level):
        node_inv = sep_inv[level]
        for side in range(2):
            weight[level, side] = dot(node_inv, sep_fac[level, side]).astype(BF16)
        free[level] = dot(node_inv, sep_rhs[level])

    loads["sep_fac"].wait()
    loads["sep_rhs"].wait()
    loads["sep_inv"].wait()
    for level in range(depth):
        prepare(level)

    for level in range(depth):
        stride = 2 ** max(level - 1, 0)
        p = lax.rem(lax.div(me, stride), 2)
        near, far = 1 - p, p
        for j in range(CHUNKS):
            columns = slice(j * width, (j + 1) * width)
            if level == 0:
                total = dot(weight[level, 1], edge[j])
                arrived(level, 0, j)
                total += dot(weight[level, 0], recv[level, 0, j])
            else:
                arrived(level, near, j)
                if level == relay_level:
                    beyond = lax.rem(me + 2 * stride + (n - 4 * stride) * p, n)
                    send(recv.at[level, near, j], level, far, j, beyond, 1)
                total = dot(weight[level, near], recv[level, near, j])
                arrived(level, far, j)
                total += dot(weight[level, far], recv[level, far, j])
            sol[level, j] = (free[level, :, columns] - total).astype(BF16)
            if level + 1 < depth:
                step = 2**level
                q = lax.rem(lax.div(me, step), 2)
                up, down = peer(step), peer(-step)
                if level + 1 == relay_level:
                    send(sol.at[level, j], level + 1, q, j, up + (down - up) * q, 0)
                else:
                    send(sol.at[level, j], level + 1, 1 - q, j, down + (up - down) * q, 0)
                    send(sol.at[level, j], level + 1, q, j, up + (down - up) * q, 1)
            copy = pltpu.make_async_copy(
                sol.at[level, j], sep_out.at[level, 0, :, pl.ds(j * width, width)], out_sem.at[level, j]
            )
            copy.start()
            out_copies.append(copy)
        if level == 0:
            leaf_level(top)

    for copy in sends:
        copy.wait_send()
    for copy in out_copies:
        copy.wait()


def place(leaf, sep, leaf_out, sep_out, sem):
    copies = []
    for level in range(LEAF_LEVELS):
        rows = pl.ds(level * LEVEL_ROWS, LEVEL_ROWS)
        copies.append(pltpu.make_async_copy(leaf.at[rows], leaf_out.at[rows], sem.at[level]))
    for level in range(sep.shape[0]):
        copies.append(
            pltpu.make_async_copy(sep.at[level], sep_out.at[level], sem.at[LEAF_LEVELS + level])
        )
    for copy in copies:
        copy.start()
    for copy in copies:
        copy.wait()


def shards(n, leaf_rhs, separator_rhs, leaf_inverse, leaf_factor, separator_inverse, separator_factor, block_pattern, link_row):
    depth = separator_rhs.shape[0]
    block, loads = leaf_rhs.shape[1:]
    width = loads // CHUNKS
    upper, coupled = leaf_factor.shape[:2]
    matmuls = leaf_rhs.shape[0] + upper * coupled + 5 * depth
    hbm = pl.BlockSpec(memory_space=pltpu.HBM)
    smem = pl.BlockSpec(memory_space=pltpu.SMEM)
    solved = pl.pallas_call(
        functools.partial(kernel, n, depth, -1),
        out_shape=(
            jax.ShapeDtypeStruct(leaf_rhs.shape, BF16),
            jax.ShapeDtypeStruct(separator_rhs.shape, BF16),
        ),
        in_specs=[hbm] * 6 + [smem] * 2,
        out_specs=(hbm, hbm),
        scratch_shapes=[
            pltpu.VMEM(leaf_rhs.shape, BF16),
            pltpu.VMEM(leaf_inverse.shape, BF16),
            pltpu.VMEM(leaf_factor.shape, BF16),
            pltpu.VMEM((depth, block, loads), BF16),
            pltpu.VMEM((depth, block, block), BF16),
            pltpu.VMEM((depth, 2, block, block), BF16),
            pltpu.VMEM(leaf_rhs.shape, BF16),
            pltpu.VMEM((CHUNKS, block, width), BF16),
            pltpu.VMEM((depth, 2, block, block), BF16),
            pltpu.VMEM((depth, block, loads), F32),
            pltpu.VMEM((depth, CHUNKS, block, width), BF16),
            pltpu.VMEM((depth, 2, CHUNKS, block, width), BF16),
            pltpu.SemaphoreType.DMA((3 * LEAF_LEVELS + 2,)),
            pltpu.SemaphoreType.DMA((LEAF_LEVELS,)),
            pltpu.SemaphoreType.DMA((depth, CHUNKS)),
            pltpu.SemaphoreType.DMA((depth, 2, CHUNKS)),
            pltpu.SemaphoreType.DMA((depth, 2, CHUNKS)),
        ],
        compiler_params=pltpu.CompilerParams(
            collective_id=0, has_side_effects=True, vmem_limit_bytes=64 * 2**20
        ),
        cost_estimate=pl.CostEstimate(
            flops=2 * matmuls * block * block * loads,
            bytes_accessed=2 * (matmuls + 2 * leaf_rhs.shape[0]) * block * loads,
            transcendentals=0,
        ),
        name="tree_solve",
    )(leaf_rhs, separator_rhs, leaf_inverse, leaf_factor, separator_inverse, separator_factor, block_pattern.T, link_row)
    return pl.pallas_call(
        place,
        out_shape=tuple(jax.ShapeDtypeStruct(a.shape, a.dtype) for a in solved),
        in_specs=[hbm] * 2,
        out_specs=(hbm, hbm),
        scratch_shapes=[pltpu.SemaphoreType.DMA((LEAF_LEVELS + depth,))],
        compiler_params=pltpu.CompilerParams(vmem_limit_bytes=64 * 2**20),
        name="place_results",
    )(*solved)


def solution(mesh):
    placed = (
        P("rows", None, None),
        P(None, "rows", None, None),
        P(("draws", "rows"), None, None),
        P(("draws", "rows"), None, None, None),
        P(None, ("draws", "rows"), None, None),
        P(None, ("draws", "rows"), None, None, None),
        P("rows", None),
        P("rows"),
    )
    return jax.shard_map(
        functools.partial(shards, mesh.shape["rows"]),
        mesh=mesh,
        in_specs=placed,
        out_specs=(P(("draws", "rows"), None, None), P(None, ("draws", "rows"), None, None)),
        check_vma=False,
    )
```

```python
import functools

import jax
import jax.numpy as jnp
from jax import lax
from jax.experimental import pallas as pl
from jax.experimental.pallas import tpu as pltpu
from jax.sharding import PartitionSpec as P

LEVEL_ROWS = 4
LEAF_LEVELS = 3
CHUNKS = 2
F32 = jnp.float32
BF16 = jnp.bfloat16


def dot(a, b):
    return jnp.dot(a, b, preferred_element_type=F32)


def kernel(
    n,
    depth,
    relay_level,
    rhs_hbm,
    sep_rhs_hbm,
    inv_hbm,
    fac_hbm,
    sep_inv_hbm,
    sep_fac_hbm,
    pattern,
    link,
    leaf_out,
    sep_out,
    rhs,
    inv,
    fac,
    sep_rhs,
    sep_inv,
    sep_fac,
    solved,
    edge,
    weight,
    free,
    sol,
    recv,
    load_sem,
    leaf_sem,
    out_sem,
    send_sem,
    recv_sem,
):
    me = lax.axis_index("rows")
    coupled = fac.shape[1]
    width = sol.shape[-1]

    def peer(by):
        return lax.rem(me + (by % n), n)

    loads = {}

    def load(name, src, dst):
        copy = pltpu.make_async_copy(src, dst, load_sem.at[len(loads)])
        copy.start()
        loads[name] = copy

    for level in range(LEAF_LEVELS):
        rows = pl.ds(level * LEVEL_ROWS, LEVEL_ROWS)
        if level:
            low = pl.ds((level - 1) * LEVEL_ROWS, LEVEL_ROWS)
            load(("fac", level), fac_hbm.at[low], fac.at[low])
        load(("rhs", level), rhs_hbm.at[rows], rhs.at[rows])
        load(("inv", level), inv_hbm.at[rows], inv.at[rows])
    load("sep_fac", sep_fac_hbm.at[:, 0], sep_fac)
    load("sep_rhs", sep_rhs_hbm.at[:, 0], sep_rhs)
    load("sep_inv", sep_inv_hbm.at[:, 0], sep_inv)

    offsets = sorted({(sign * 2**h) % n for h in range(depth - 1) for sign in (1, -1)})
    barrier = pltpu.get_barrier_semaphore()
    for by in offsets:
        pl.semaphore_signal(
            barrier, inc=1, device_id={"rows": peer(by)}, device_id_type=pl.DeviceIdType.MESH
        )

    def residual(row, q):
        total = dot(fac[q, 0], solved[pattern[0, q]])
        for k in range(1, coupled):
            total += dot(fac[q, k], solved[pattern[k, q]])
        return (rhs[row].astype(F32) - total).astype(BF16)

    out_copies = []

    def leaf_write(level):
        rows = pl.ds(level * LEVEL_ROWS, LEVEL_ROWS)
        copy = pltpu.make_async_copy(solved.at[rows], leaf_out.at[rows], leaf_sem.at[level])
        copy.start()
        out_copies.append(copy)

    loads[("rhs", 0)].wait()
    loads[("inv", 0)].wait()
    for row in range(LEVEL_ROWS):
        solved[row] = dot(inv[row], rhs[row]).astype(BF16)
    leaf_write(0)

    def leaf_level(level):
        first = level * LEVEL_ROWS
        parts = [residual(first + i, first - LEVEL_ROWS + i) for i in range(LEVEL_ROWS)]
        for i in range(LEVEL_ROWS):
            solved[first + i] = dot(inv[first + i], parts[i]).astype(BF16)
        leaf_write(level)

    for level in range(1, LEAF_LEVELS - 1):
        for name in ("fac", "rhs", "inv"):
            loads[(name, level)].wait()
        leaf_level(level)

    top = LEAF_LEVELS - 1
    for name in ("fac", "rhs", "inv"):
        loads[(name, top)].wait()
    link_row = link[0]
    edge_block = dot(inv[link_row], residual(link_row, jnp.maximum(link_row - LEVEL_ROWS, 0))).astype(BF16)
    for j in range(CHUNKS):
        edge[j] = edge_block[:, j * width : (j + 1) * width]

    pl.semaphore_wait(barrier, len(offsets))

    sends = []

    def send(src, level, side, j, to, slot):
        copy = pltpu.make_async_remote_copy(
            src_ref=src,
            dst_ref=recv.at[level, side, j],
            send_sem=send_sem.at[level, slot, j],
            recv_sem=recv_sem.at[level, side, j],
            device_id={"rows": to},
            device_id_type=pl.DeviceIdType.MESH,
        )
        copy.start()
        sends.append(copy)

    def arrived(level, side, j):
        pltpu.make_async_remote_copy(
            src_ref=edge.at[j],
            dst_ref=recv.at[level, side, j],
            send_sem=send_sem.at[level, 0, j],
            recv_sem=recv_sem.at[level, side, j],
            device_id={"rows": peer(1)},
            device_id_type=pl.DeviceIdType.MESH,
        ).wait_recv()

    for j in range(CHUNKS):
        send(edge.at[j], 0, 0, j, peer(1), 0)

    def prepare(level):
        node_inv = sep_inv[level]
        for side in range(2):
            weight[level, side] = dot(node_inv, sep_fac[level, side]).astype(BF16)
        free[level] = dot(node_inv, sep_rhs[level])

    loads["sep_fac"].wait()
    loads["sep_rhs"].wait()
    loads["sep_inv"].wait()
    for level in range(depth):
        prepare(level)

    for level in range(depth):
        stride = 2 ** max(level - 1, 0)
        p = lax.rem(lax.div(me, stride), 2)
        near, far = 1 - p, p
        for j in range(CHUNKS):
            columns = slice(j * width, (j + 1) * width)
            if level == 0:
                total = dot(weight[level, 1], edge[j])
                arrived(level, 0, j)
                total += dot(weight[level, 0], recv[level, 0, j])
            else:
                arrived(level, near, j)
                if level == relay_level:
                    beyond = lax.rem(me + 2 * stride + (n - 4 * stride) * p, n)
                    send(recv.at[level, near, j], level, far, j, beyond, 1)
                total = dot(weight[level, near], recv[level, near, j])
                arrived(level, far, j)
                total += dot(weight[level, far], recv[level, far, j])
            sol[level, j] = (free[level, :, columns] - total).astype(BF16)
            if level + 1 < depth:
                step = 2**level
                q = lax.rem(lax.div(me, step), 2)
                up, down = peer(step), peer(-step)
                if level + 1 == relay_level:
                    send(sol.at[level, j], level + 1, q, j, up + (down - up) * q, 0)
                else:
                    send(sol.at[level, j], level + 1, 1 - q, j, down + (up - down) * q, 0)
                    send(sol.at[level, j], level + 1, q, j, up + (down - up) * q, 1)
            copy = pltpu.make_async_copy(
                sol.at[level, j], sep_out.at[level, 0, :, pl.ds(j * width, width)], out_sem.at[level, j]
            )
            copy.start()
            out_copies.append(copy)
        if level == 0:
            leaf_level(top)

    for copy in sends:
        copy.wait_send()
    for copy in out_copies:
        copy.wait()


def place(leaf, sep, leaf_out, sep_out, leaf_held, sep_held, in_sem, out_sem):
    pieces = [
        (leaf.at[rows], leaf_held.at[rows], leaf_out.at[rows])
        for rows in (pl.ds(i, 2) for i in range(0, leaf.shape[0], 2))
    ] + [(sep.at[i], sep_held.at[i], sep_out.at[i]) for i in range(sep.shape[0])]
    loads = [
        pltpu.make_async_copy(src, held, in_sem.at[i]) for i, (src, held, _) in enumerate(pieces)
    ]
    stores = [
        pltpu.make_async_copy(held, dst, out_sem.at[i]) for i, (_, held, dst) in enumerate(pieces)
    ]
    for copy in loads:
        copy.start()
    for copy_in, copy_out in zip(loads, stores):
        copy_in.wait()
        copy_out.start()
    for copy in stores:
        copy.wait()


def shards(n, leaf_rhs, separator_rhs, leaf_inverse, leaf_factor, separator_inverse, separator_factor, block_pattern, link_row):
    depth = separator_rhs.shape[0]
    block, loads = leaf_rhs.shape[1:]
    width = loads // CHUNKS
    upper, coupled = leaf_factor.shape[:2]
    matmuls = leaf_rhs.shape[0] + upper * coupled + 5 * depth
    hbm = pl.BlockSpec(memory_space=pltpu.HBM)
    smem = pl.BlockSpec(memory_space=pltpu.SMEM)
    solved = pl.pallas_call(
        functools.partial(kernel, n, depth, -1),
        out_shape=(
            jax.ShapeDtypeStruct(leaf_rhs.shape, BF16),
            jax.ShapeDtypeStruct(separator_rhs.shape, BF16),
        ),
        in_specs=[hbm] * 6 + [smem] * 2,
        out_specs=(hbm, hbm),
        scratch_shapes=[
            pltpu.VMEM(leaf_rhs.shape, BF16),
            pltpu.VMEM(leaf_inverse.shape, BF16),
            pltpu.VMEM(leaf_factor.shape, BF16),
            pltpu.VMEM((depth, block, loads), BF16),
            pltpu.VMEM((depth, block, block), BF16),
            pltpu.VMEM((depth, 2, block, block), BF16),
            pltpu.VMEM(leaf_rhs.shape, BF16),
            pltpu.VMEM((CHUNKS, block, width), BF16),
            pltpu.VMEM((depth, 2, block, block), BF16),
            pltpu.VMEM((depth, block, loads), F32),
            pltpu.VMEM((depth, CHUNKS, block, width), BF16),
            pltpu.VMEM((depth, 2, CHUNKS, block, width), BF16),
            pltpu.SemaphoreType.DMA((3 * LEAF_LEVELS + 2,)),
            pltpu.SemaphoreType.DMA((LEAF_LEVELS,)),
            pltpu.SemaphoreType.DMA((depth, CHUNKS)),
            pltpu.SemaphoreType.DMA((depth, 2, CHUNKS)),
            pltpu.SemaphoreType.DMA((depth, 2, CHUNKS)),
        ],
        compiler_params=pltpu.CompilerParams(
            collective_id=0, has_side_effects=True, vmem_limit_bytes=64 * 2**20
        ),
        cost_estimate=pl.CostEstimate(
            flops=2 * matmuls * block * block * loads,
            bytes_accessed=2 * (matmuls + 2 * leaf_rhs.shape[0]) * block * loads,
            transcendentals=0,
        ),
        name="tree_solve",
    )(leaf_rhs, separator_rhs, leaf_inverse, leaf_factor, separator_inverse, separator_factor, block_pattern.T, link_row)
    return pl.pallas_call(
        place,
        out_shape=tuple(jax.ShapeDtypeStruct(a.shape, a.dtype) for a in solved),
        in_specs=[hbm] * 2,
        out_specs=(hbm, hbm),
        scratch_shapes=[
            pltpu.VMEM(leaf_rhs.shape, BF16),
            pltpu.VMEM(separator_rhs.shape, BF16),
            pltpu.SemaphoreType.DMA((leaf_rhs.shape[0] // 2 + depth,)),
            pltpu.SemaphoreType.DMA((leaf_rhs.shape[0] // 2 + depth,)),
        ],
        compiler_params=pltpu.CompilerParams(vmem_limit_bytes=64 * 2**20),
        name="place_results",
    )(*solved)


def solution(mesh):
    placed = (
        P("rows", None, None),
        P(None, "rows", None, None),
        P(("draws", "rows"), None, None),
        P(("draws", "rows"), None, None, None),
        P(None, ("draws", "rows"), None, None),
        P(None, ("draws", "rows"), None, None, None),
        P("rows", None),
        P("rows"),
    )
    return jax.shard_map(
        functools.partial(shards, mesh.shape["rows"]),
        mesh=mesh,
        in_specs=placed,
        out_specs=(P(("draws", "rows"), None, None), P(None, ("draws", "rows"), None, None)),
        check_vma=False,
    )
```

```python
import functools

import jax
import jax.numpy as jnp
from jax import lax
from jax.experimental import pallas as pl
from jax.experimental.pallas import tpu as pltpu
from jax.sharding import PartitionSpec as P

LEVEL_ROWS = 4
LEAF_LEVELS = 3
CHUNKS = 4
PAIR = 2
F32 = jnp.float32
BF16 = jnp.bfloat16


def dot(a, b):
    return jnp.dot(a, b, preferred_element_type=F32)


def kernel(
    n,
    depth,
    relay_level,
    rhs_hbm,
    sep_rhs_hbm,
    inv_hbm,
    fac_hbm,
    sep_inv_hbm,
    sep_fac_hbm,
    pattern,
    link,
    leaf_out,
    sep_out,
    rhs,
    inv,
    fac,
    sep_rhs,
    sep_inv,
    sep_fac,
    solved,
    edge,
    weight,
    free,
    sol,
    turned,
    recv,
    load_sem,
    leaf_sem,
    out_sem,
    send_sem,
    recv_sem,
):
    me = lax.axis_index("rows")
    coupled = fac.shape[1]
    width = sol.shape[1] // CHUNKS

    def peer(by):
        return lax.rem(me + (by % n), n)

    loads = {}

    def load(name, src, dst):
        copy = pltpu.make_async_copy(src, dst, load_sem.at[len(loads)])
        copy.start()
        loads[name] = copy

    for level in range(LEAF_LEVELS):
        rows = pl.ds(level * LEVEL_ROWS, LEVEL_ROWS)
        if level:
            low = pl.ds((level - 1) * LEVEL_ROWS, LEVEL_ROWS)
            load(("fac", level), fac_hbm.at[low], fac.at[low])
        load(("rhs", level), rhs_hbm.at[rows], rhs.at[rows])
        load(("inv", level), inv_hbm.at[rows], inv.at[rows])
    load("sep_fac", sep_fac_hbm.at[:, 0], sep_fac)
    load("sep_rhs", sep_rhs_hbm.at[:, 0], sep_rhs)
    load("sep_inv", sep_inv_hbm.at[:, 0], sep_inv)

    offsets = sorted({(sign * 2**h) % n for h in range(depth - 1) for sign in (1, -1)})
    barrier = pltpu.get_barrier_semaphore()
    for by in offsets:
        pl.semaphore_signal(
            barrier, inc=1, device_id={"rows": peer(by)}, device_id_type=pl.DeviceIdType.MESH
        )

    def residual(row, q):
        total = dot(fac[q, 0], solved[pattern[0, q]])
        for k in range(1, coupled):
            total += dot(fac[q, k], solved[pattern[k, q]])
        return (rhs[row].astype(F32) - total).astype(BF16)

    out_copies = []

    def leaf_write(level):
        rows = pl.ds(level * LEVEL_ROWS, LEVEL_ROWS)
        copy = pltpu.make_async_copy(solved.at[rows], leaf_out.at[rows], leaf_sem.at[level])
        copy.start()
        out_copies.append(copy)

    loads[("rhs", 0)].wait()
    loads[("inv", 0)].wait()
    for row in range(LEVEL_ROWS):
        solved[row] = dot(inv[row], rhs[row]).astype(BF16)
    leaf_write(0)

    def leaf_level(level):
        first = level * LEVEL_ROWS
        parts = [residual(first + i, first - LEVEL_ROWS + i) for i in range(LEVEL_ROWS)]
        for i in range(LEVEL_ROWS):
            solved[first + i] = dot(inv[first + i], parts[i]).astype(BF16)
        leaf_write(level)

    for level in range(1, LEAF_LEVELS - 1):
        for name in ("fac", "rhs", "inv"):
            loads[(name, level)].wait()
        leaf_level(level)

    top = LEAF_LEVELS - 1
    for name in ("fac", "rhs", "inv"):
        loads[(name, top)].wait()
    link_row = link[0]
    edge_block = dot(inv[link_row], residual(link_row, jnp.maximum(link_row - LEVEL_ROWS, 0)))
    edge[...] = edge_block.T.astype(BF16)

    pl.semaphore_wait(barrier, len(offsets))

    def chunk(j):
        return pl.ds(j * width, width)

    sends = []

    def send(src, level, side, j, to, slot):
        copy = pltpu.make_async_remote_copy(
            src_ref=src,
            dst_ref=recv.at[level, side, chunk(j)],
            send_sem=send_sem.at[level, slot, j],
            recv_sem=recv_sem.at[level, side, j],
            device_id={"rows": to},
            device_id_type=pl.DeviceIdType.MESH,
        )
        copy.start()
        sends.append(copy)

    def arrived(level, side, j):
        pltpu.make_async_remote_copy(
            src_ref=edge.at[chunk(j)],
            dst_ref=recv.at[level, side, chunk(j)],
            send_sem=send_sem.at[level, 0, j],
            recv_sem=recv_sem.at[level, side, j],
            device_id={"rows": peer(1)},
            device_id_type=pl.DeviceIdType.MESH,
        ).wait_recv()

    for j in range(CHUNKS):
        send(edge.at[chunk(j)], 0, 0, j, peer(1), 0)

    def prepare(level):
        node_inv = sep_inv[level]
        for side in range(2):
            weight[level, side] = dot(node_inv, sep_fac[level, side]).T.astype(BF16)
        free[level] = dot(node_inv, sep_rhs[level]).T

    loads["sep_fac"].wait()
    loads["sep_rhs"].wait()
    loads["sep_inv"].wait()
    for level in range(2):
        prepare(level)

    def sep_write(level, pair):
        lanes = PAIR * width
        turned[level, pair] = sol[level, pl.ds(pair * lanes, lanes)].astype(F32).T.astype(BF16)
        copy = pltpu.make_async_copy(
            turned.at[level, pair],
            sep_out.at[level, 0, :, pl.ds(pair * lanes, lanes)],
            out_sem.at[level, pair],
        )
        copy.start()
        out_copies.append(copy)

    for level in range(depth):
        stride = 2 ** max(level - 1, 0)
        p = lax.rem(lax.div(me, stride), 2)
        near, far = 1 - p, p
        for j in range(CHUNKS):
            here = chunk(j)
            if level == 0:
                total = dot(edge[here], weight[level, 1])
                arrived(level, 0, j)
                total += dot(recv[level, 0, here], weight[level, 0])
            else:
                arrived(level, near, j)
                if level == relay_level:
                    beyond = lax.rem(me + 2 * stride + (n - 4 * stride) * p, n)
                    send(recv.at[level, near, here], level, far, j, beyond, 1)
                total = dot(recv[level, near, here], weight[level, near])
                arrived(level, far, j)
                total += dot(recv[level, far, here], weight[level, far])
            sol[level, here] = (free[level, here] - total).astype(BF16)
            if level + 1 < depth:
                step = 2**level
                q = lax.rem(lax.div(me, step), 2)
                up, down = peer(step), peer(-step)
                if level + 1 == relay_level:
                    send(sol.at[level, here], level + 1, q, j, up + (down - up) * q, 0)
                else:
                    send(sol.at[level, here], level + 1, 1 - q, j, down + (up - down) * q, 0)
                    send(sol.at[level, here], level + 1, q, j, up + (down - up) * q, 1)
            if level + 1 == depth and j % PAIR == PAIR - 1:
                sep_write(level, j // PAIR)
        if level == 0:
            leaf_level(top)
            for later in range(2, depth):
                prepare(later)
        if level + 1 < depth:
            for pair in range(CHUNKS // PAIR):
                sep_write(level, pair)

    for copy in sends:
        copy.wait_send()
    for copy in out_copies:
        copy.wait()


def place(leaf, sep, leaf_out, sep_out, leaf_held, sep_held, in_sem, out_sem):
    pieces = [
        (leaf.at[rows], leaf_held.at[rows], leaf_out.at[rows])
        for rows in (pl.ds(i, 2) for i in range(0, leaf.shape[0], 2))
    ] + [(sep.at[i], sep_held.at[i], sep_out.at[i]) for i in range(sep.shape[0])]
    loads = [
        pltpu.make_async_copy(src, held, in_sem.at[i]) for i, (src, held, _) in enumerate(pieces)
    ]
    stores = [
        pltpu.make_async_copy(held, dst, out_sem.at[i]) for i, (_, held, dst) in enumerate(pieces)
    ]
    for copy in loads:
        copy.start()
    for copy_in, copy_out in zip(loads, stores):
        copy_in.wait()
        copy_out.start()
    for copy in stores:
        copy.wait()


def shards(n, leaf_rhs, separator_rhs, leaf_inverse, leaf_factor, separator_inverse, separator_factor, block_pattern, link_row):
    depth = separator_rhs.shape[0]
    block, loads = leaf_rhs.shape[1:]
    width = loads // CHUNKS
    upper, coupled = leaf_factor.shape[:2]
    matmuls = leaf_rhs.shape[0] + upper * coupled + 5 * depth
    hbm = pl.BlockSpec(memory_space=pltpu.HBM)
    smem = pl.BlockSpec(memory_space=pltpu.SMEM)
    solved = pl.pallas_call(
        functools.partial(kernel, n, depth, -1),
        out_shape=(
            jax.ShapeDtypeStruct(leaf_rhs.shape, BF16),
            jax.ShapeDtypeStruct(separator_rhs.shape, BF16),
        ),
        in_specs=[hbm] * 6 + [smem] * 2,
        out_specs=(hbm, hbm),
        scratch_shapes=[
            pltpu.VMEM(leaf_rhs.shape, BF16),
            pltpu.VMEM(leaf_inverse.shape, BF16),
            pltpu.VMEM(leaf_factor.shape, BF16),
            pltpu.VMEM((depth, block, loads), BF16),
            pltpu.VMEM((depth, block, block), BF16),
            pltpu.VMEM((depth, 2, block, block), BF16),
            pltpu.VMEM(leaf_rhs.shape, BF16),
            pltpu.VMEM((loads, block), BF16),
            pltpu.VMEM((depth, 2, block, block), BF16),
            pltpu.VMEM((depth, loads, block), F32),
            pltpu.VMEM((depth, loads, block), BF16),
            pltpu.VMEM((depth, CHUNKS // PAIR, block, PAIR * width), BF16),
            pltpu.VMEM((depth, 2, loads, block), BF16),
            pltpu.SemaphoreType.DMA((3 * LEAF_LEVELS + 2,)),
            pltpu.SemaphoreType.DMA((LEAF_LEVELS,)),
            pltpu.SemaphoreType.DMA((depth, CHUNKS // PAIR)),
            pltpu.SemaphoreType.DMA((depth, 2, CHUNKS)),
            pltpu.SemaphoreType.DMA((depth, 2, CHUNKS)),
        ],
        compiler_params=pltpu.CompilerParams(
            collective_id=0, has_side_effects=True, vmem_limit_bytes=64 * 2**20
        ),
        cost_estimate=pl.CostEstimate(
            flops=2 * matmuls * block * block * loads,
            bytes_accessed=2 * (matmuls + 2 * leaf_rhs.shape[0]) * block * loads,
            transcendentals=0,
        ),
        name="tree_solve",
    )(leaf_rhs, separator_rhs, leaf_inverse, leaf_factor, separator_inverse, separator_factor, block_pattern.T, link_row)
    return pl.pallas_call(
        place,
        out_shape=tuple(jax.ShapeDtypeStruct(a.shape, a.dtype) for a in solved),
        in_specs=[hbm] * 2,
        out_specs=(hbm, hbm),
        scratch_shapes=[
            pltpu.VMEM(leaf_rhs.shape, BF16),
            pltpu.VMEM(separator_rhs.shape, BF16),
            pltpu.SemaphoreType.DMA((leaf_rhs.shape[0] // 2 + depth,)),
            pltpu.SemaphoreType.DMA((leaf_rhs.shape[0] // 2 + depth,)),
        ],
        compiler_params=pltpu.CompilerParams(vmem_limit_bytes=64 * 2**20),
        name="place_results",
    )(*solved)


def solution(mesh):
    placed = (
        P("rows", None, None),
        P(None, "rows", None, None),
        P(("draws", "rows"), None, None),
        P(("draws", "rows"), None, None, None),
        P(None, ("draws", "rows"), None, None),
        P(None, ("draws", "rows"), None, None, None),
        P("rows", None),
        P("rows"),
    )
    return jax.shard_map(
        functools.partial(shards, mesh.shape["rows"]),
        mesh=mesh,
        in_specs=placed,
        out_specs=(P(("draws", "rows"), None, None), P(None, ("draws", "rows"), None, None)),
        check_vma=False,
    )
```

```python
import functools

import jax
import jax.numpy as jnp
from jax import lax
from jax.experimental import pallas as pl
from jax.experimental.pallas import tpu as pltpu
from jax.sharding import PartitionSpec as P

LEVEL_ROWS = 4
LEAF_LEVELS = 3
CHUNKS = 2
F32 = jnp.float32
BF16 = jnp.bfloat16


def dot(a, b):
    return jnp.dot(a, b, preferred_element_type=F32)


def kernel(
    n,
    depth,
    relay_level,
    rhs_hbm,
    sep_rhs_hbm,
    inv_hbm,
    fac_hbm,
    sep_inv_hbm,
    sep_fac_hbm,
    pattern,
    link,
    leaf_out,
    sep_out,
    rhs,
    inv,
    fac,
    sep_rhs,
    sep_inv,
    sep_fac,
    solved,
    edge,
    weight,
    free,
    sol,
    recv,
    weight_above,
    sent_rest,
    load_sem,
    leaf_sem,
    out_sem,
    send_sem,
    recv_sem,
    above_sem,
):
    me = lax.axis_index("rows")
    coupled = fac.shape[1]
    width = sol.shape[-1]

    def peer(by):
        return lax.rem(me + (by % n), n)

    loads = {}

    def load(name, src, dst):
        copy = pltpu.make_async_copy(src, dst, load_sem.at[len(loads)])
        copy.start()
        loads[name] = copy

    def load_nodes(name, levels):
        load(("sep_inv", name), sep_inv_hbm.at[levels, 0], sep_inv.at[levels])
        load(("sep_fac", name), sep_fac_hbm.at[levels, 0], sep_fac.at[levels])
        load(("sep_rhs", name), sep_rhs_hbm.at[levels, 0], sep_rhs.at[levels])

    def wait_nodes(name):
        for what in ("sep_inv", "sep_fac", "sep_rhs"):
            loads[(what, name)].wait()

    for level in range(LEAF_LEVELS):
        rows = pl.ds(level * LEVEL_ROWS, LEVEL_ROWS)
        if level:
            low = pl.ds((level - 1) * LEVEL_ROWS, LEVEL_ROWS)
            load(("fac", level), fac_hbm.at[low], fac.at[low])
        load(("rhs", level), rhs_hbm.at[rows], rhs.at[rows])
        load(("inv", level), inv_hbm.at[rows], inv.at[rows])
        if level == 0:
            load_nodes("first", pl.ds(0, 1))
    load_nodes("rest", pl.ds(1, depth - 1))

    offsets = sorted({(sign * 2**h) % n for h in range(depth - 1) for sign in (1, -1)})
    barrier = pltpu.get_barrier_semaphore()
    for by in offsets:
        pl.semaphore_signal(
            barrier, inc=1, device_id={"rows": peer(by)}, device_id_type=pl.DeviceIdType.MESH
        )

    def residual(row, q):
        total = dot(fac[q, 0], solved[pattern[0, q]])
        for k in range(1, coupled):
            total += dot(fac[q, k], solved[pattern[k, q]])
        return (rhs[row].astype(F32) - total).astype(BF16)

    out_copies = []

    def leaf_write(level):
        rows = pl.ds(level * LEVEL_ROWS, LEVEL_ROWS)
        copy = pltpu.make_async_copy(solved.at[rows], leaf_out.at[rows], leaf_sem.at[level])
        copy.start()
        out_copies.append(copy)

    loads[("rhs", 0)].wait()
    loads[("inv", 0)].wait()
    for row in range(LEVEL_ROWS):
        solved[row] = dot(inv[row], rhs[row]).astype(BF16)
    leaf_write(0)

    def leaf_level(level):
        first = level * LEVEL_ROWS
        parts = [residual(first + i, first - LEVEL_ROWS + i) for i in range(LEVEL_ROWS)]
        for i in range(LEVEL_ROWS):
            solved[first + i] = dot(inv[first + i], parts[i]).astype(BF16)
        leaf_write(level)

    for level in range(1, LEAF_LEVELS - 1):
        for name in ("fac", "rhs", "inv"):
            loads[(name, level)].wait()
        leaf_level(level)

    def prepare(level):
        node_inv = sep_inv[level]
        for side in range(2):
            weight[level, side] = dot(node_inv, sep_fac[level, side]).astype(BF16)
        free[level] = dot(node_inv, sep_rhs[level])

    wait_nodes("first")
    prepare(0)

    pl.semaphore_wait(barrier, len(offsets))
    weight_copy = pltpu.make_async_remote_copy(
        src_ref=weight.at[0, 0],
        dst_ref=weight_above,
        send_sem=above_sem.at[0],
        recv_sem=above_sem.at[1],
        device_id={"rows": peer(-1)},
        device_id_type=pl.DeviceIdType.MESH,
    )
    weight_copy.start()

    top = LEAF_LEVELS - 1
    for name in ("fac", "rhs", "inv"):
        loads[(name, top)].wait()
    link_row = link[0]
    edge_block = dot(inv[link_row], residual(link_row, jnp.maximum(link_row - LEVEL_ROWS, 0))).astype(BF16)
    for j in range(CHUNKS):
        edge[j] = edge_block[:, j * width : (j + 1) * width]

    sends = []

    def send(src, level, side, j, to, slot):
        copy = pltpu.make_async_remote_copy(
            src_ref=src,
            dst_ref=recv.at[level, side, j],
            send_sem=send_sem.at[level, slot, j],
            recv_sem=recv_sem.at[level, side, j],
            device_id={"rows": to},
            device_id_type=pl.DeviceIdType.MESH,
        )
        copy.start()
        sends.append(copy)

    def arrived(level, side, j):
        pltpu.make_async_remote_copy(
            src_ref=edge.at[j],
            dst_ref=recv.at[level, side, j],
            send_sem=send_sem.at[level, 0, j],
            recv_sem=recv_sem.at[level, side, j],
            device_id={"rows": peer(1)},
            device_id_type=pl.DeviceIdType.MESH,
        ).wait_recv()

    for j in range(CHUNKS):
        send(edge.at[j], 0, 0, j, peer(1), 0)
        columns = slice(j * width, (j + 1) * width)
        rest = free[0, :, columns] - dot(weight[0, 1], edge[j])
        free[0, :, columns] = rest
        sent_rest[j] = rest.astype(BF16)
        send(sent_rest.at[j], 1, 1, j, peer(-1), 1)

    for level in range(depth):
        stride = 2 ** max(level - 1, 0)
        p = lax.rem(lax.div(me, stride), 2)
        near, far = 1 - p, p
        for j in range(CHUNKS):
            columns = slice(j * width, (j + 1) * width)
            if level == 0:
                arrived(level, 0, j)
                total = dot(weight[level, 0], recv[level, 0, j])
            elif level == 1:
                arrived(level, 1, j)
                above = recv[level, 1, j].astype(F32) - dot(weight_above[...], edge[j])
                total = dot(weight[level, 1], above.astype(BF16))
                arrived(level, 0, j)
                total += dot(weight[level, 0], recv[level, 0, j])
            else:
                arrived(level, near, j)
                if level == relay_level:
                    beyond = lax.rem(me + 2 * stride + (n - 4 * stride) * p, n)
                    send(recv.at[level, near, j], level, far, j, beyond, 1)
                total = dot(weight[level, near], recv[level, near, j])
                arrived(level, far, j)
                total += dot(weight[level, far], recv[level, far, j])
            sol[level, j] = (free[level, :, columns] - total).astype(BF16)
            if level + 1 < depth:
                step = 2**level
                q = lax.rem(lax.div(me, step), 2)
                up, down = peer(step), peer(-step)
                if level == 0:
                    send(sol.at[level, j], 1, 0, j, up, 0)
                elif level + 1 == relay_level:
                    send(sol.at[level, j], level + 1, q, j, up + (down - up) * q, 0)
                else:
                    send(sol.at[level, j], level + 1, 1 - q, j, down + (up - down) * q, 0)
                    send(sol.at[level, j], level + 1, q, j, up + (down - up) * q, 1)
            copy = pltpu.make_async_copy(
                sol.at[level, j], sep_out.at[level, 0, :, pl.ds(j * width, width)], out_sem.at[level, j]
            )
            copy.start()
            out_copies.append(copy)
        if level == 0:
            wait_nodes("rest")
        if level + 1 < depth:
            prepare(level + 1)
        if level == 0:
            weight_copy.wait()
        if level == 1:
            leaf_level(top)

    for copy in sends:
        copy.wait_send()
    for copy in out_copies:
        copy.wait()


def place(leaf, sep, leaf_out, sep_out, leaf_held, sep_held, in_sem, out_sem):
    pieces = [
        (leaf.at[rows], leaf_held.at[rows], leaf_out.at[rows])
        for rows in (pl.ds(i, 2) for i in range(0, leaf.shape[0], 2))
    ] + [(sep.at[i], sep_held.at[i], sep_out.at[i]) for i in range(sep.shape[0])]
    loads = [
        pltpu.make_async_copy(src, held, in_sem.at[i]) for i, (src, held, _) in enumerate(pieces)
    ]
    stores = [
        pltpu.make_async_copy(held, dst, out_sem.at[i]) for i, (_, held, dst) in enumerate(pieces)
    ]
    for copy in loads:
        copy.start()
    for copy_in, copy_out in zip(loads, stores):
        copy_in.wait()
        copy_out.start()
    for copy in stores:
        copy.wait()


def shards(n, leaf_rhs, separator_rhs, leaf_inverse, leaf_factor, separator_inverse, separator_factor, block_pattern, link_row):
    depth = separator_rhs.shape[0]
    block, loads = leaf_rhs.shape[1:]
    width = loads // CHUNKS
    upper, coupled = leaf_factor.shape[:2]
    matmuls = leaf_rhs.shape[0] + upper * coupled + 5 * depth
    hbm = pl.BlockSpec(memory_space=pltpu.HBM)
    smem = pl.BlockSpec(memory_space=pltpu.SMEM)
    solved = pl.pallas_call(
        functools.partial(kernel, n, depth, -1),
        out_shape=(
            jax.ShapeDtypeStruct(leaf_rhs.shape, BF16),
            jax.ShapeDtypeStruct(separator_rhs.shape, BF16),
        ),
        in_specs=[hbm] * 6 + [smem] * 2,
        out_specs=(hbm, hbm),
        scratch_shapes=[
            pltpu.VMEM(leaf_rhs.shape, BF16),
            pltpu.VMEM(leaf_inverse.shape, BF16),
            pltpu.VMEM(leaf_factor.shape, BF16),
            pltpu.VMEM((depth, block, loads), BF16),
            pltpu.VMEM((depth, block, block), BF16),
            pltpu.VMEM((depth, 2, block, block), BF16),
            pltpu.VMEM(leaf_rhs.shape, BF16),
            pltpu.VMEM((CHUNKS, block, width), BF16),
            pltpu.VMEM((depth, 2, block, block), BF16),
            pltpu.VMEM((depth, block, loads), F32),
            pltpu.VMEM((depth, CHUNKS, block, width), BF16),
            pltpu.VMEM((depth, 2, CHUNKS, block, width), BF16),
            pltpu.VMEM((block, block), BF16),
            pltpu.VMEM((CHUNKS, block, width), BF16),
            pltpu.SemaphoreType.DMA((3 * LEAF_LEVELS + 5,)),
            pltpu.SemaphoreType.DMA((LEAF_LEVELS,)),
            pltpu.SemaphoreType.DMA((depth, CHUNKS)),
            pltpu.SemaphoreType.DMA((depth, 2, CHUNKS)),
            pltpu.SemaphoreType.DMA((depth, 2, CHUNKS)),
            pltpu.SemaphoreType.DMA((2,)),
        ],
        compiler_params=pltpu.CompilerParams(
            collective_id=0, has_side_effects=True, vmem_limit_bytes=64 * 2**20
        ),
        cost_estimate=pl.CostEstimate(
            flops=2 * matmuls * block * block * loads,
            bytes_accessed=2 * (matmuls + 2 * leaf_rhs.shape[0]) * block * loads,
            transcendentals=0,
        ),
        name="tree_solve",
    )(leaf_rhs, separator_rhs, leaf_inverse, leaf_factor, separator_inverse, separator_factor, block_pattern.T, link_row)
    return pl.pallas_call(
        place,
        out_shape=tuple(jax.ShapeDtypeStruct(a.shape, a.dtype) for a in solved),
        in_specs=[hbm] * 2,
        out_specs=(hbm, hbm),
        scratch_shapes=[
            pltpu.VMEM(leaf_rhs.shape, BF16),
            pltpu.VMEM(separator_rhs.shape, BF16),
            pltpu.SemaphoreType.DMA((leaf_rhs.shape[0] // 2 + depth,)),
            pltpu.SemaphoreType.DMA((leaf_rhs.shape[0] // 2 + depth,)),
        ],
        compiler_params=pltpu.CompilerParams(vmem_limit_bytes=64 * 2**20),
        name="place_results",
    )(*solved)


def solution(mesh):
    placed = (
        P("rows", None, None),
        P(None, "rows", None, None),
        P(("draws", "rows"), None, None),
        P(("draws", "rows"), None, None, None),
        P(None, ("draws", "rows"), None, None),
        P(None, ("draws", "rows"), None, None, None),
        P("rows", None),
        P("rows"),
    )
    return jax.shard_map(
        functools.partial(shards, mesh.shape["rows"]),
        mesh=mesh,
        in_specs=placed,
        out_specs=(P(("draws", "rows"), None, None), P(None, ("draws", "rows"), None, None)),
        check_vma=False,
    )
```

```python
import functools

import jax
import jax.numpy as jnp
from jax import lax
from jax.experimental import pallas as pl
from jax.experimental.pallas import tpu as pltpu
from jax.sharding import PartitionSpec as P

LEVEL_ROWS = 4
LEAF_LEVELS = 3
CHUNKS = 2
F32 = jnp.float32
BF16 = jnp.bfloat16


def dot(a, b):
    return jnp.dot(a, b, preferred_element_type=F32)


def kernel(
    n,
    depth,
    relay_level,
    rhs_hbm,
    sep_rhs_hbm,
    inv_hbm,
    fac_hbm,
    sep_inv_hbm,
    sep_fac_hbm,
    pattern,
    link,
    leaf_out,
    sep_out,
    rhs,
    inv,
    fac,
    sep_rhs,
    sep_inv,
    sep_fac,
    solved,
    edge,
    weight,
    free,
    sol,
    recv,
    load_sem,
    leaf_sem,
    out_sem,
    send_sem,
    recv_sem,
):
    me = lax.axis_index("rows")
    coupled = fac.shape[1]
    width = sol.shape[-1]

    def peer(by):
        return lax.rem(me + (by % n), n)

    loads = {}

    def load(name, src, dst):
        copy = pltpu.make_async_copy(src, dst, load_sem.at[len(loads)])
        copy.start()
        loads[name] = copy

    def load_nodes(name, levels):
        load(("sep_inv", name), sep_inv_hbm.at[levels, 0], sep_inv.at[levels])
        load(("sep_fac", name), sep_fac_hbm.at[levels, 0], sep_fac.at[levels])
        load(("sep_rhs", name), sep_rhs_hbm.at[levels, 0], sep_rhs.at[levels])

    def wait_nodes(name):
        for what in ("sep_inv", "sep_fac", "sep_rhs"):
            loads[(what, name)].wait()

    for level in range(LEAF_LEVELS):
        rows = pl.ds(level * LEVEL_ROWS, LEVEL_ROWS)
        if level:
            low = pl.ds((level - 1) * LEVEL_ROWS, LEVEL_ROWS)
            load(("fac", level), fac_hbm.at[low], fac.at[low])
        load(("rhs", level), rhs_hbm.at[rows], rhs.at[rows])
        load(("inv", level), inv_hbm.at[rows], inv.at[rows])
        if level == 0:
            load_nodes("first", pl.ds(0, 1))
    load_nodes("rest", pl.ds(1, depth - 1))

    offsets = sorted({(sign * 2**h) % n for h in range(depth - 1) for sign in (1, -1)})
    barrier = pltpu.get_barrier_semaphore()
    for by in offsets:
        pl.semaphore_signal(
            barrier, inc=1, device_id={"rows": peer(by)}, device_id_type=pl.DeviceIdType.MESH
        )

    def residual(row, q):
        total = dot(fac[q, 0], solved[pattern[0, q]])
        for k in range(1, coupled):
            total += dot(fac[q, k], solved[pattern[k, q]])
        return (rhs[row].astype(F32) - total).astype(BF16)

    out_copies = []

    def leaf_write(level):
        rows = pl.ds(level * LEVEL_ROWS, LEVEL_ROWS)
        copy = pltpu.make_async_copy(solved.at[rows], leaf_out.at[rows], leaf_sem.at[level])
        copy.start()
        out_copies.append(copy)

    loads[("rhs", 0)].wait()
    loads[("inv", 0)].wait()
    for row in range(LEVEL_ROWS):
        solved[row] = dot(inv[row], rhs[row]).astype(BF16)
    leaf_write(0)

    def leaf_level(level):
        first = level * LEVEL_ROWS
        parts = [residual(first + i, first - LEVEL_ROWS + i) for i in range(LEVEL_ROWS)]
        for i in range(LEVEL_ROWS):
            solved[first + i] = dot(inv[first + i], parts[i]).astype(BF16)
        leaf_write(level)

    for level in range(1, LEAF_LEVELS - 1):
        for name in ("fac", "rhs", "inv"):
            loads[(name, level)].wait()
        leaf_level(level)

    def prepare(level):
        node_inv = sep_inv[level]
        for side in range(2):
            weight[level, side] = dot(node_inv, sep_fac[level, side]).astype(BF16)
        free[level] = dot(node_inv, sep_rhs[level])

    wait_nodes("first")
    prepare(0)

    top = LEAF_LEVELS - 1
    for name in ("fac", "rhs", "inv"):
        loads[(name, top)].wait()
    link_row = link[0]
    edge_block = dot(inv[link_row], residual(link_row, jnp.maximum(link_row - LEVEL_ROWS, 0))).astype(BF16)
    for j in range(CHUNKS):
        edge[j] = edge_block[:, j * width : (j + 1) * width]

    pl.semaphore_wait(barrier, len(offsets))

    sends = []

    def send(src, level, side, j, to, slot):
        copy = pltpu.make_async_remote_copy(
            src_ref=src,
            dst_ref=recv.at[level, side, j],
            send_sem=send_sem.at[level, slot, j],
            recv_sem=recv_sem.at[level, side, j],
            device_id={"rows": to},
            device_id_type=pl.DeviceIdType.MESH,
        )
        copy.start()
        sends.append(copy)

    def arrived(level, side, j):
        pltpu.make_async_remote_copy(
            src_ref=edge.at[j],
            dst_ref=recv.at[level, side, j],
            send_sem=send_sem.at[level, 0, j],
            recv_sem=recv_sem.at[level, side, j],
            device_id={"rows": peer(1)},
            device_id_type=pl.DeviceIdType.MESH,
        ).wait_recv()

    for j in range(CHUNKS):
        send(edge.at[j], 0, 0, j, peer(1), 0)

    for level in range(depth):
        stride = 2 ** max(level - 1, 0)
        p = lax.rem(lax.div(me, stride), 2)
        near, far = 1 - p, p
        for j in range(CHUNKS):
            columns = slice(j * width, (j + 1) * width)
            if level == 0:
                total = dot(weight[level, 1], edge[j])
                arrived(level, 0, j)
                total += dot(weight[level, 0], recv[level, 0, j])
            else:
                arrived(level, near, j)
                if level == relay_level:
                    beyond = lax.rem(me + 2 * stride + (n - 4 * stride) * p, n)
                    send(recv.at[level, near, j], level, far, j, beyond, 1)
                total = dot(weight[level, near], recv[level, near, j])
                arrived(level, far, j)
                total += dot(weight[level, far], recv[level, far, j])
            sol[level, j] = (free[level, :, columns] - total).astype(BF16)
            if level + 1 < depth:
                step = 2**level
                q = lax.rem(lax.div(me, step), 2)
                up, down = peer(step), peer(-step)
                if level + 1 == relay_level:
                    send(sol.at[level, j], level + 1, q, j, up + (down - up) * q, 0)
                else:
                    send(sol.at[level, j], level + 1, 1 - q, j, down + (up - down) * q, 0)
                    send(sol.at[level, j], level + 1, q, j, up + (down - up) * q, 1)
            copy = pltpu.make_async_copy(
                sol.at[level, j], sep_out.at[level, 0, :, pl.ds(j * width, width)], out_sem.at[level, j]
            )
            copy.start()
            out_copies.append(copy)
        if level == 0:
            wait_nodes("rest")
        if level + 1 < depth:
            prepare(level + 1)
        if level == 1:
            leaf_level(top)

    for copy in sends:
        copy.wait_send()
    for copy in out_copies:
        copy.wait()


def place(leaf, sep, leaf_out, sep_out, leaf_held, sep_held, in_sem, out_sem):
    pieces = [
        (leaf.at[rows], leaf_held.at[rows], leaf_out.at[rows])
        for rows in (pl.ds(i, 2) for i in range(0, leaf.shape[0], 2))
    ] + [(sep.at[i], sep_held.at[i], sep_out.at[i]) for i in range(sep.shape[0])]
    loads = [
        pltpu.make_async_copy(src, held, in_sem.at[i]) for i, (src, held, _) in enumerate(pieces)
    ]
    stores = [
        pltpu.make_async_copy(held, dst, out_sem.at[i]) for i, (_, held, dst) in enumerate(pieces)
    ]
    for copy in loads:
        copy.start()
    for copy_in, copy_out in zip(loads, stores):
        copy_in.wait()
        copy_out.start()
    for copy in stores:
        copy.wait()


def shards(n, leaf_rhs, separator_rhs, leaf_inverse, leaf_factor, separator_inverse, separator_factor, block_pattern, link_row):
    depth = separator_rhs.shape[0]
    block, loads = leaf_rhs.shape[1:]
    width = loads // CHUNKS
    upper, coupled = leaf_factor.shape[:2]
    matmuls = leaf_rhs.shape[0] + upper * coupled + 5 * depth
    hbm = pl.BlockSpec(memory_space=pltpu.HBM)
    smem = pl.BlockSpec(memory_space=pltpu.SMEM)
    solved = pl.pallas_call(
        functools.partial(kernel, n, depth, -1),
        out_shape=(
            jax.ShapeDtypeStruct(leaf_rhs.shape, BF16),
            jax.ShapeDtypeStruct(separator_rhs.shape, BF16),
        ),
        in_specs=[hbm] * 6 + [smem] * 2,
        out_specs=(hbm, hbm),
        scratch_shapes=[
            pltpu.VMEM(leaf_rhs.shape, BF16),
            pltpu.VMEM(leaf_inverse.shape, BF16),
            pltpu.VMEM(leaf_factor.shape, BF16),
            pltpu.VMEM((depth, block, loads), BF16),
            pltpu.VMEM((depth, block, block), BF16),
            pltpu.VMEM((depth, 2, block, block), BF16),
            pltpu.VMEM(leaf_rhs.shape, BF16),
            pltpu.VMEM((CHUNKS, block, width), BF16),
            pltpu.VMEM((depth, 2, block, block), BF16),
            pltpu.VMEM((depth, block, loads), F32),
            pltpu.VMEM((depth, CHUNKS, block, width), BF16),
            pltpu.VMEM((depth, 2, CHUNKS, block, width), BF16),
            pltpu.SemaphoreType.DMA((3 * LEAF_LEVELS + 5,)),
            pltpu.SemaphoreType.DMA((LEAF_LEVELS,)),
            pltpu.SemaphoreType.DMA((depth, CHUNKS)),
            pltpu.SemaphoreType.DMA((depth, 2, CHUNKS)),
            pltpu.SemaphoreType.DMA((depth, 2, CHUNKS)),
        ],
        compiler_params=pltpu.CompilerParams(
            collective_id=0, has_side_effects=True, vmem_limit_bytes=64 * 2**20
        ),
        cost_estimate=pl.CostEstimate(
            flops=2 * matmuls * block * block * loads,
            bytes_accessed=2 * (matmuls + 2 * leaf_rhs.shape[0]) * block * loads,
            transcendentals=0,
        ),
        name="tree_solve",
    )(leaf_rhs, separator_rhs, leaf_inverse, leaf_factor, separator_inverse, separator_factor, block_pattern.T, link_row)
    return pl.pallas_call(
        place,
        out_shape=tuple(jax.ShapeDtypeStruct(a.shape, a.dtype) for a in solved),
        in_specs=[hbm] * 2,
        out_specs=(hbm, hbm),
        scratch_shapes=[
            pltpu.VMEM(leaf_rhs.shape, BF16),
            pltpu.VMEM(separator_rhs.shape, BF16),
            pltpu.SemaphoreType.DMA((leaf_rhs.shape[0] // 2 + depth,)),
            pltpu.SemaphoreType.DMA((leaf_rhs.shape[0] // 2 + depth,)),
        ],
        compiler_params=pltpu.CompilerParams(vmem_limit_bytes=64 * 2**20),
        name="place_results",
    )(*solved)


def solution(mesh):
    placed = (
        P("rows", None, None),
        P(None, "rows", None, None),
        P(("draws", "rows"), None, None),
        P(("draws", "rows"), None, None, None),
        P(None, ("draws", "rows"), None, None),
        P(None, ("draws", "rows"), None, None, None),
        P("rows", None),
        P("rows"),
    )
    return jax.shard_map(
        functools.partial(shards, mesh.shape["rows"]),
        mesh=mesh,
        in_specs=placed,
        out_specs=(P(("draws", "rows"), None, None), P(None, ("draws", "rows"), None, None)),
        check_vma=False,
    )
```
